32 devices in a mesh: ctx: 8 (over z, x), tp: 4 (over y, core).
Axes of the slice: x: 2, y: 2, z: 4, core: 2. Of those that a mesh axis runs over, the one named last changes fastest.
Arguments:
- queries: bfloat16 [256, 8192], P('ctx', 'tp'), may hold values from -6 to 6
- cache_keys: bfloat16 [32768, 1024], P('ctx', 'tp'), may hold values from -18 to 18
- cache_values: bfloat16 [32768, 1024], P('ctx', 'tp'), may hold values from -6 to 6
- span_keys: bfloat16 [256, 1024], P('ctx', 'tp'), may hold values from -24 to 24
- span_values: bfloat16 [256, 1024], P('ctx', 'tp'), may hold values from -6 to 6
- out_weight: bfloat16 [8192, 8192], P('tp', 'ctx'), may hold values from -0.0625 to 0.0625
- residual: bfloat16 [256, 8192], P('tp', 'ctx'), may hold values from -72 to 72
- norm_gain: bfloat16 [8192], P('ctx'), may hold values from 0.5 to 1.5
- head_weight: bfloat16 [8192, 128256], P(None, ('ctx', 'tp')), may hold values from -0.198873782 to 0.198873782
- targets: int32 [256], replicated, may hold values from 0 to 128255
- window_lengths: int32 [4], replicated, may hold values from 1 to 128, 256 in all
Outputs:
- token_logprob: float32 [256], P('ctx')
- window_means: float32 [4], replicated
The draws below stay inside these ranges and needn't reach their ends.
Inputs may be any that keep to these rules, and one draw needn't show every extreme that they name: `window_lengths`: the 4 lengths sum to 256.
All inputs are finite; a program needn't handle non-finite values.
Results may differ from the reference program's by a relative error of at most 0.0025.
Values may be sent and summed in bfloat16 or wider, within the bound.
A program may use at most 128 MiB of HBM per device.

```python
import math
import jax
import jax.numpy as jnp
import numpy as np
from jax import lax

D = 8192
HEADS = 64
KV_HEADS = 8
HD = 128
VOCAB = 128256
WINDOW = 128
SPAN = 256
PREFIX = 32768
WINDOWS = 4


def draw_cache_keys(key, part):
    drawn = 3.0 * jnp.clip(jax.random.normal(jax.random.fold_in(key, 11), (PREFIX, KV_HEADS * HD), jnp.float32), -6.0, 6.0)
    return drawn.astype(jnp.bfloat16)


def draw_queries(key, part):
    drawn = jnp.clip(jax.random.normal(jax.random.fold_in(key, 12), (SPAN, HEADS * HD), jnp.float32), -6.0, 6.0)
    return drawn.astype(jnp.bfloat16)


def draw_head_weight(key, part):
    scaling = 3.0 * D ** (-0.5)
    drawn = scaling * jnp.clip(jax.random.normal(jax.random.fold_in(key, 13), (D, VOCAB), jnp.float32), -6.0, 6.0)
    return drawn.astype(jnp.bfloat16)


def draw_residual(key, part):
    column_scale = 0.6 + 1.2 * jnp.arange(D, dtype=jnp.float32) / (D - 1)
    drawn = jnp.clip(jax.random.normal(jax.random.fold_in(key, 14), (SPAN, D), jnp.float32), -4.0, 4.0) * column_scale[None, :]
    return drawn.astype(jnp.bfloat16)


def place_ends(drawn, stream_key, low, largest):
    index_at = [jax.random.randint(jax.random.fold_in(stream_key, axis), (), 0, length) for axis, length in enumerate(drawn.shape)]
    longest = drawn.shape.index(max(drawn.shape))
    neighbour = index_at[:longest] + [(index_at[longest] + 1) % drawn.shape[longest]] + index_at[longest + 1:]
    return drawn.at[tuple(index_at)].set(low).at[tuple(neighbour)].set(largest)


def level_of(key, dims, cuts, smallest, largest):
    level = 1.0
    for axis_at, shards_of in cuts:
        steps = jax.random.uniform(jax.random.fold_in(jax.random.fold_in(key, 6), axis_at), (shards_of,), jnp.float32, smallest / len(cuts), largest / len(cuts))
        level = level * jnp.repeat(jnp.exp(steps), dims[axis_at] // shards_of).reshape((-1,) + (1,) * (len(dims) - 1 - axis_at))
    return level


def wide_ids(key, dims, number_of, lean):
    portions = [min(1 << octave, number_of + 1 - (1 << octave)) * (1 << 20) // math.isqrt((1 << octave) ** lean) + 1 for octave in range((number_of + 1).bit_length()) if 1 << octave <= number_of]
    width = 1 + sum(portions) // (1 << 30)
    table = np.cumsum(np.array([max(1, weight // width) for weight in portions]))
    pick = jax.random.randint(jax.random.fold_in(key, 1), dims, 0, int(table[len(portions) - 1]))
    start = jnp.left_shift(1, jnp.searchsorted(jnp.asarray(table, jnp.int32), pick, side="right").astype(jnp.int32))
    standing = start - 1 + jax.random.randint(jax.random.fold_in(key, 4), dims, 0, 1 << 30) % jnp.minimum(start, number_of + 1 - start)
    return jax.random.permutation(jax.random.fold_in(key, 2), number_of)[standing].astype(jnp.int32)


def length_profile(count, total, limit, skew):
    portions = [(1 << 20) // math.isqrt(standing ** skew) + 1 for standing in range(2, count + 1)]
    spare, counts = total - limit - (count - 1), [1] * (count - 1)
    while spare > 0:
        movable = [i for i in range(count - 1) if counts[i] < limit]
        mass, budget = sum([portions[i] for i in movable]), spare
        for i in movable:
            more = min(limit - counts[i], max(1, budget * portions[i] // mass), spare)
            counts[i] = counts[i] + more
            spare = spare - more
    return np.array([limit] + counts)


def ragged_sizes(key, count, total, limit, slope):
    if count == 2:
        one = jax.random.randint(key, (), max(1, total - limit), min(limit, total - 1) + 1)
        return jnp.stack([one, total - one])
    tallies = jnp.asarray(length_profile(count, total, limit, slope), jnp.int32)
    couples = (count - 1) // 2
    source_of, receiver = tallies[1:1 + 2 * couples:2], tallies[2:2 + 2 * couples:2]
    room = jnp.minimum(source_of - 1, limit - receiver)
    shifted = jax.random.randint(jax.random.fold_in(key, 1), (couples,), 0, 1 << 20) % (room + 1)
    tallies = tallies.at[1:1 + 2 * couples:2].set(source_of - shifted).at[2:2 + 2 * couples:2].set(receiver + shifted)
    return tallies[jax.random.permutation(jax.random.fold_in(key, 2), count)]


def noise(rng, extent, scale, bound, split=(), held_as=jnp.bfloat16):
    level = level_of(rng, extent, split, -0.22, 0.18) if split else 1.0
    entries = jax.random.normal(rng, extent, jnp.float32) * scale * level
    return jnp.minimum(jnp.maximum(entries, -bound), bound).astype(held_as)


def setup_inputs(seed: int = 0) -> dict:
    streams_of = jax.random.split(jax.random.key(seed), 12)
    queries = draw_queries(jax.random.fold_in(streams_of[11], 71), 0)
    cache_keys = draw_cache_keys(jax.random.fold_in(streams_of[11], 71), 0)
    cache_values = noise(streams_of[2], (PREFIX, KV_HEADS * HD), 1.0, 6.0, ((0, 8), (1, 4)))
    span_keys = noise(streams_of[3], (SPAN, KV_HEADS * HD), 4.0, 24.0, ((0, 8), (1, 4)))
    span_values = noise(streams_of[4], (SPAN, KV_HEADS * HD), 1.0, 6.0, ((0, 8), (1, 4)))
    out_weight = noise(streams_of[5], (HEADS * HD, D), (HEADS * HD) ** -0.5, 0.0625, ((0, 4), (1, 8)))
    residual = draw_residual(jax.random.fold_in(streams_of[11], 71), 0)
    norm_gain = jnp.clip(1.0 + 0.1 * jax.random.normal(streams_of[7], (D,), jnp.float32), 0.5, 1.5).astype(jnp.bfloat16)
    head_weight = draw_head_weight(jax.random.fold_in(streams_of[11], 71), 0)
    targets = place_ends(wide_ids(streams_of[9], (SPAN,), VOCAB, 2), jax.random.fold_in(streams_of[9], 3), 0, VOCAB - 1).astype(jnp.int32)
    window_lengths = ragged_sizes(streams_of[10], WINDOWS, SPAN, WINDOW, 1).astype(jnp.int32)
    return {"queries": queries, "cache_keys": cache_keys, "cache_values": cache_values, "span_keys": span_keys, "span_values": span_values, "out_weight": out_weight, "residual": residual, "norm_gain": norm_gain, "head_weight": head_weight, "targets": targets, "window_lengths": window_lengths}


EPSILON = 1e-05
NEGATIVE = -1e+30

def fold_block(state, scores, value_rows):
    row_max, row_sum, weighted = state
    new_max = jnp.maximum(row_max, lax.optimization_barrier(jnp.max(scores, axis=1)))
    fading = jnp.exp(row_max - new_max)
    weights = jnp.exp(scores - new_max[:, None])
    row_sum = row_sum * fading + lax.optimization_barrier(jnp.sum(weights, axis=1))
    weighted = weighted * fading[:, None] + jnp.dot(weights.astype(jnp.bfloat16), value_rows, preferred_element_type=jnp.float32)
    return (new_max, row_sum, weighted)

def attend_head(bundle):
    query_rows, cache_part, value_part, fresh_keys, fresh_values = bundle
    row_count = query_rows.shape[0]
    scaling = HD ** (-0.5)
    block_size = min(1024, cache_part.shape[0])
    block_count = cache_part.shape[0] // block_size
    key_blocks = cache_part.reshape(block_count, block_size, HD)
    value_blocks = value_part.reshape(block_count, block_size, HD)

    def advance(state, block_pair):
        scores = jnp.dot(query_rows, block_pair[0].T, preferred_element_type=jnp.float32) * scaling
        return (fold_block(state, scores, block_pair[1]), None)
    start_state = (jnp.full((row_count,), NEGATIVE, jnp.float32), jnp.zeros((row_count,), jnp.float32), jnp.zeros((row_count, HD), jnp.float32))
    state, unused = lax.scan(advance, start_state, (key_blocks, value_blocks))
    scores = jnp.dot(query_rows, fresh_keys.T, preferred_element_type=jnp.float32) * scaling
    token_of_row = jnp.arange(row_count, dtype=jnp.int32) % SPAN
    key_token = jnp.arange(fresh_keys.shape[0], dtype=jnp.int32)
    scores = jnp.where(token_of_row[:, None] >= key_token[None, :], scores, NEGATIVE)
    row_max, row_sum, weighted = fold_block(state, scores, fresh_values)
    return (weighted / row_sum[:, None]).astype(jnp.bfloat16)

def reference(queries, cache_keys, cache_values, span_keys, span_values, out_weight, residual, norm_gain, head_weight, targets, window_lengths):
    group_size = HEADS // KV_HEADS
    query_heads = queries.reshape(SPAN, KV_HEADS, group_size, HD).transpose(1, 2, 0, 3).reshape(KV_HEADS, group_size * SPAN, HD)
    key_heads = cache_keys.reshape(PREFIX, KV_HEADS, HD).transpose(1, 0, 2)
    value_heads = cache_values.reshape(PREFIX, KV_HEADS, HD).transpose(1, 0, 2)
    fresh_key_heads = span_keys.reshape(SPAN, KV_HEADS, HD).transpose(1, 0, 2)
    fresh_value_heads = span_values.reshape(SPAN, KV_HEADS, HD).transpose(1, 0, 2)
    attended = lax.map(attend_head, (query_heads, key_heads, value_heads, fresh_key_heads, fresh_value_heads))
    attended = attended.reshape(KV_HEADS, group_size, SPAN, HD).transpose(2, 0, 1, 3).reshape(SPAN, HEADS * HD)
    stream = residual.astype(jnp.float32) + jnp.dot(attended, out_weight, preferred_element_type=jnp.float32)
    mean_square = lax.optimization_barrier(jnp.mean(stream * stream, axis=1))
    normed = (stream * lax.rsqrt(mean_square + EPSILON)[:, None] * norm_gain.astype(jnp.float32)[None, :]).astype(jnp.bfloat16)
    logits = jnp.dot(normed, head_weight, preferred_element_type=jnp.float32)
    row_max = lax.optimization_barrier(jnp.max(logits, axis=1))
    log_total = row_max + jnp.log(lax.optimization_barrier(jnp.sum(jnp.exp(logits - row_max[:, None]), axis=1)))
    target_logit = jnp.take_along_axis(logits, targets[:, None].astype(jnp.int32), axis=1)[:, 0]
    token_logprob = target_logit - log_total
    window_ends = jnp.cumsum(window_lengths).astype(jnp.int32)
    window_starts = window_ends - window_lengths
    positions = jnp.arange(SPAN, dtype=jnp.int32)
    member = ((positions[None, :] >= window_starts[:, None]) & (positions[None, :] < window_ends[:, None])).astype(jnp.float32)
    window_sums = jnp.dot(member, token_logprob, precision=lax.Precision.HIGHEST)
    window_means = window_sums / window_lengths.astype(jnp.float32)
    return (token_logprob, window_means)
```

```python
import functools

import jax
import jax.numpy as jnp
from jax import lax
from jax.experimental import pallas as pl
from jax.experimental.pallas import tpu as pltpu
from jax.sharding import PartitionSpec as P

HD = 128
GROUP = 8
EPSILON = 1e-05
NEGATIVE = -1e30
MESH = pl.DeviceIdType.MESH
F32 = jnp.float32
BF16 = jnp.bfloat16


def dot_nt(left, right):
    return lax.dot_general(
        left, right, (((1,), (1,)), ((), ())), preferred_element_type=F32
    )


def remote(src, dst, send_sem, recv_sem, device):
    return pltpu.make_async_remote_copy(
        src_ref=src,
        dst_ref=dst,
        send_sem=send_sem,
        recv_sem=recv_sem,
        device_id=device,
        device_id_type=MESH,
    )


def kernel(
    n_ctx,
    n_tp,
    slots,
    chunk,
    query_ref,
    key_ref,
    value_ref,
    fresh_key_ref,
    fresh_value_ref,
    residual_ref,
    gain_ref,
    target_ref,
    out_weight_ref,
    head_ref,
    result_ref,
    q_buf,
    o_send,
    s_send,
    o_buf,
    s_buf,
    a_buf,
    w_buf,
    p_send,
    p_buf,
    y_buf,
    sq_buf,
    column_buf,
    h_buf,
    acc,
    st_buf,
    q_ss,
    q_rs,
    o_ss,
    o_rs,
    s_ss,
    s_rs,
    a_ss,
    a_rs,
    p_ss,
    p_rs,
    y_ss,
    y_rs,
    sq_ss,
    sq_rs,
    st_ss,
    st_rs,
    w_sem,
    h_sem,
):
    c = lax.axis_index("ctx")
    t = lax.axis_index("tp")
    n_dev = n_ctx * n_tp
    me = c * n_tp + t
    kv_local = key_ref.shape[1] // HD
    span_dev = query_ref.shape[0]
    rows = span_dev * GROUP
    keys = key_ref.shape[0]
    tok_tp = residual_ref.shape[0]
    cols = residual_ref.shape[1]
    vocab_dev, width = head_ref.shape
    n_tokens = n_ctx * span_dev
    chunks = width // chunk
    half = tok_tp // 2
    scaling = HD ** (-0.5)

    def fetch(j, slot):
        return pltpu.make_async_copy(
            head_ref.at[:, pl.ds(pl.multiple_of(j * chunk, chunk), chunk)],
            h_buf.at[slot],
            h_sem.at[slot],
        )

    w_copy = pltpu.make_async_copy(out_weight_ref, w_buf, w_sem)
    w_copy.start()
    for j in range(slots):
        fetch(j, j).start()

    def other(step):
        index = lax.rem(me + step, n_dev)
        return (index // n_tp, lax.rem(index, n_tp))

    barrier = pltpu.get_barrier_semaphore()

    @pl.loop(1, n_dev)
    def _(step):
        pl.semaphore_signal(barrier, inc=1, device_id=other(step), device_id_type=MESH)

    pl.semaphore_wait(barrier, n_dev - 1)

    def peer(step):
        away = ((step + 1) // 2) * (2 * lax.rem(step, 2) - 1)
        return lax.rem(c + away + n_ctx, n_ctx)

    def query_copy(src_rank, dst):
        return remote(
            q_buf.at[src_rank], q_buf.at[src_rank], q_ss.at[dst], q_rs.at[src_rank], (dst, t)
        )

    def partial_copies(rank, dst):
        return (
            remote(o_send.at[dst], o_buf.at[rank], o_ss.at[dst], o_rs.at[rank], (dst, t)),
            remote(s_send.at[dst], s_buf.at[rank], s_ss.at[dst], s_rs.at[rank], (dst, t)),
        )

    for kv in range(kv_local):
        for g in range(GROUP):
            lo = (kv * GROUP + g) * HD
            q_buf[c, kv, g * span_dev : (g + 1) * span_dev, :] = query_ref[:, lo : lo + HD]

    @pl.loop(1, n_ctx)
    def _(step):
        query_copy(c, peer(step)).start()

    key_block = min(1024, keys)

    @pl.loop(0, n_ctx)
    def _(step):
        p = peer(step)

        @pl.when(step > 0)
        def _():
            query_copy(p, p).wait_recv()

        for kv in range(kv_local):
            lo = kv * HD
            q = q_buf[p, kv]
            row_max = None
            for b in range(keys // key_block + 1):
                if b < keys // key_block:
                    at = b * key_block
                    s = dot_nt(key_ref[at : at + key_block, lo : lo + HD], q)
                    v = value_ref[lo : lo + HD, at : at + key_block]
                else:
                    s = dot_nt(fresh_key_ref[:, lo : lo + HD], q)
                    j = lax.broadcasted_iota(jnp.int32, s.shape, 0)
                    token = lax.rem(
                        lax.broadcasted_iota(jnp.int32, s.shape, 1), span_dev
                    )
                    seen = (p * span_dev + token >= c * span_dev + j) & (j < span_dev)
                    s = jnp.where(seen, s, NEGATIVE)
                    v = fresh_value_ref[lo : lo + HD, :]
                top = jnp.max(s, axis=0, keepdims=True)
                if row_max is None:
                    new_max = top
                else:
                    new_max = jnp.maximum(row_max, top)
                w = jnp.exp((s - new_max) * scaling)
                part_sum = jnp.sum(w, axis=0, keepdims=True)
                part = jnp.dot(v, w.astype(BF16), preferred_element_type=F32)
                if row_max is None:
                    row_sum, weighted = part_sum, part
                else:
                    fading = jnp.exp((row_max - new_max) * scaling)
                    row_sum = row_sum * fading + part_sum
                    weighted = weighted * fading + part
                row_max = new_max
            o_send[p, kv] = (weighted / row_sum).astype(BF16)
            s_send[p, kv, 0:4, :] = jnp.broadcast_to(row_max * scaling, (4, rows))
            s_send[p, kv, 4:8, :] = jnp.broadcast_to(row_sum, (4, rows))

        @pl.when(step > 0)
        def _():
            for copy in partial_copies(c, p):
                copy.start()

    o_buf[c] = o_send[c]
    s_buf[c] = s_send[c]

    @pl.loop(1, n_ctx)
    def _(step):
        p = peer(step)
        query_copy(c, p).wait_send()
        for copy in partial_copies(p, p):
            copy.wait_send()
            copy.wait_recv()

    for kv in range(kv_local):
        tops = [s_buf[src, kv, 0:1, :] for src in range(n_ctx)]
        best = functools.reduce(jnp.maximum, tops)
        total = jnp.zeros((1, rows), F32)
        mixed = jnp.zeros((HD, rows), F32)
        for src in range(n_ctx):
            share = s_buf[src, kv, 4:5, :] * jnp.exp(tops[src] - best)
            total = total + share
            mixed = mixed + o_buf[src, kv].astype(F32) * share
        attended = (mixed / total).T.astype(BF16)
        for g in range(GROUP):
            lo = (kv * GROUP + g) * HD
            a_buf[c, :, lo : lo + HD] = attended[g * span_dev : (g + 1) * span_dev]

    def attended_copy(rank, dst):
        return remote(a_buf.at[rank], a_buf.at[rank], a_ss.at[dst], a_rs.at[rank], (dst, t))

    @pl.loop(1, n_ctx)
    def _(step):
        attended_copy(c, peer(step)).start()

    w_copy.wait()

    @pl.loop(1, n_ctx)
    def _(step):
        attended_copy(peer(step), peer(step)).wait_recv()

    tile = min(256, cols)
    for at in range(0, cols, tile):
        product = jnp.dot(
            a_buf[...].reshape(n_tokens, a_buf.shape[2]),
            w_buf[:, at : at + tile],
            preferred_element_type=F32,
        ).astype(BF16)
        p_send[:, :, at : at + tile] = product.reshape(n_tp, tok_tp, tile)

    def product_copy(rank, dst):
        return remote(p_send.at[dst], p_buf.at[rank], p_ss.at[dst], p_rs.at[rank], (c, dst))

    for step in range(1, n_tp):
        product_copy(t, lax.rem(t + step, n_tp)).start()
    p_buf[t] = p_send[t]
    for step in range(1, n_tp):
        dst = lax.rem(t + step, n_tp)
        product_copy(dst, dst).wait_recv()

    stream = residual_ref[...].astype(F32)
    for src in range(n_tp):
        stream = stream + p_buf[src].astype(F32)
    gained = (stream * gain_ref[...].astype(F32)).astype(BF16)
    y_buf[c, t, 0] = gained[:half]
    y_buf[c, t, 1] = gained[half:]
    squares = jnp.sum(stream * stream, axis=1, keepdims=True)
    column_buf[...] = jnp.zeros(column_buf.shape, F32)
    column_buf[pl.ds(pl.multiple_of(t * tok_tp, tok_tp), tok_tp), :] = jnp.broadcast_to(
        squares, (tok_tp, 128)
    )
    sq_buf[me] = column_buf[...].T[0:8]

    n_o = n_ctx // 2
    n_y = n_tp // 2
    o, i = c // 2, lax.rem(c, 2)
    y, k = t // 2, lax.rem(t, 2)
    sent = []

    def block_copy(cc, tt, h, device, sem):
        return remote(
            y_buf.at[cc, tt, h],
            y_buf.at[cc, tt, h],
            y_ss.at[sem],
            y_rs.at[(cc * n_tp + tt) * 2 + h],
            device,
        )

    def send(cc, tt, h, device):
        copy = block_copy(cc, tt, h, device, len(sent))
        copy.start()
        sent.append(copy)

    def arrive(cc, tt, h):
        block_copy(cc, tt, h, across, 0).wait_recv()

    across = (o * 2 + (1 - i), t)
    sides = [lax.rem(y + dy, n_y) * 2 + k for dy in range(1, n_y)]
    twin = (c, y * 2 + (1 - k))
    line = [lax.rem(o + dz, n_o) * 2 + i for dz in range(n_o)]
    line_across = [lax.rem(o + dz, n_o) * 2 + (1 - i) for dz in range(n_o)]

    def forward(cc):
        send(cc, t, 0, across)
        for side in sides:
            send(cc, t, 1, (c, side))
        for h in range(2):
            send(cc, t, h, twin)

    for cc in line[1:]:
        for h in range(2):
            send(c, t, h, (cc, t))
    forward(c)

    def square_copy(rank, step, device):
        return remote(sq_buf.at[rank], sq_buf.at[rank], sq_ss.at[step], sq_rs.at[rank], device)

    @pl.loop(1, n_dev)
    def _(step):
        square_copy(me, step, other(step)).start()

    for cc in line[1:]:
        for h in range(2):
            arrive(cc, t, h)
        forward(cc)
    for cc in line:
        for side in sides:
            send(cc, t, 0, (c, side))
        send(cc, t, 1, across)
    for dz in range(n_o):
        arrive(line_across[dz], t, 0)
        for side in sides:
            send(line_across[dz], t, 0, (c, side))
        send(line_across[dz], t, 0, twin)
        for side in sides:
            arrive(line[dz], side, 1)
            send(line[dz], side, 1, across)
            send(line[dz], side, 1, twin)
    for dz in range(n_o):
        for side in sides:
            arrive(line[dz], side, 0)
            send(line[dz], side, 0, twin)
        arrive(line_across[dz], t, 1)
        send(line_across[dz], t, 1, twin)
    for dz in range(n_o):
        for side in sides:
            for h in range(2):
                arrive(line_across[dz], side, h)
                send(line_across[dz], side, h, twin)
    for cc in range(n_ctx):
        for yy in range(n_y):
            for h in range(2):
                arrive(cc, yy * 2 + (1 - k), h)

    per_source = cols // chunk

    @pl.loop(0, chunks)
    def _(j):
        slot = lax.rem(j, slots)
        fetch(j, slot).wait()
        left = y_buf[
            j // per_source, :, :, :, pl.ds(pl.multiple_of(lax.rem(j, per_source) * chunk, chunk), chunk)
        ].reshape(n_tokens, chunk)
        for at in range(0, vocab_dev, 512):
            to = min(at + 512, vocab_dev)
            product = dot_nt(h_buf[slot, at:to, :], left)

            @pl.when(j == 0)
            def _():
                acc[at:to, :] = product

            @pl.when(j > 0)
            def _():
                acc[at:to, :] += product

        @pl.when(j + slots < chunks)
        def _():
            fetch(j + slots, slot).start()

    @pl.loop(1, n_dev)
    def _(step):
        square_copy(lax.rem(me + step, n_dev), step, other(step)).wait_recv()

    vocab_start = me * vocab_dev
    total = sq_buf[0, 0:1]
    for rank in range(1, n_dev):
        total = total + sq_buf[rank, 0:1]
    scale = lax.rsqrt(total / width + EPSILON)
    top = jnp.max(acc[...] * scale, axis=0, keepdims=True)
    mass = jnp.zeros((1, n_tokens), F32)
    mark = jnp.zeros((1, n_tokens), F32)
    for at in range(0, vocab_dev, 512):
        to = min(at + 512, vocab_dev)
        logits = acc[at:to, :] * scale
        mass = mass + jnp.sum(jnp.exp(logits - top), axis=0, keepdims=True)
        entry = vocab_start + at + lax.broadcasted_iota(jnp.int32, logits.shape, 0)
        hit = target_ref[...] == entry
        mark = mark + jnp.sum(jnp.where(hit, logits, 0.0), axis=0, keepdims=True)
    st_buf[me, 0:2, :] = jnp.broadcast_to(top, (2, n_tokens))
    st_buf[me, 2:4, :] = jnp.broadcast_to(mass, (2, n_tokens))
    st_buf[me, 4:8, :] = jnp.broadcast_to(mark, (4, n_tokens))

    def stat_copy(rank, step, device):
        return remote(st_buf.at[rank], st_buf.at[rank], st_ss.at[step], st_rs.at[rank], device)

    @pl.loop(1, n_dev)
    def _(step):
        stat_copy(me, step, other(step)).start()

    for copy in sent:
        copy.wait_send()

    @pl.loop(1, n_ctx)
    def _(step):
        attended_copy(c, peer(step)).wait_send()

    for step in range(1, n_tp):
        product_copy(t, lax.rem(t + step, n_tp)).wait_send()

    @pl.loop(1, n_dev)
    def _(step):
        square_copy(me, step, other(step)).wait_send()
        stat_copy(me, step, other(step)).wait_send()
        stat_copy(lax.rem(me + step, n_dev), step, other(step)).wait_recv()

    tops = [st_buf[rank, 0:1, :] for rank in range(n_dev)]
    top = functools.reduce(jnp.maximum, tops)
    mass = jnp.zeros((1, n_tokens), F32)
    mark = jnp.zeros((1, n_tokens), F32)
    for rank in range(n_dev):
        mass = mass + st_buf[rank, 2:3, :] * jnp.exp(tops[rank] - top)
        mark = mark + st_buf[rank, 4:5, :]
    result_ref[...] = jnp.broadcast_to(mark - (top + jnp.log(mass)), result_ref.shape)


def local(
    n_ctx,
    n_tp,
    queries,
    cache_keys,
    cache_values,
    span_keys,
    span_values,
    out_weight,
    residual,
    norm_gain,
    head_weight,
    targets,
    window_lengths,
):
    span_dev = queries.shape[0]
    kv_local = cache_keys.shape[1] // HD
    rows = GROUP * span_dev
    span_total = span_dev * n_ctx
    n_dev = n_ctx * n_tp
    heads_width = queries.shape[1]
    tok_tp, cols = residual.shape
    vocab_dev = head_weight.shape[1]
    chunk = min(512, cols)
    slots = 6
    padding = max(128 - span_dev, 0)
    fresh_keys = jnp.pad(span_keys, ((0, padding), (0, 0)))
    fresh_values = jnp.pad(span_values, ((0, padding), (0, 0))).T
    vmem = pl.BlockSpec(memory_space=pltpu.VMEM)
    hbm = pl.BlockSpec(memory_space=pl.ANY)
    dma = pltpu.SemaphoreType.DMA
    n_o, n_y = n_ctx // 2, n_tp // 2
    y_sends = (
        2 * (n_o - 1)
        + n_o * (1 + n_y)
        + (n_y - 1) * 3 * n_o
        + 2 * n_ctx * n_y
    )
    table = pl.pallas_call(
        functools.partial(kernel, n_ctx, n_tp, slots, chunk),
        out_shape=jax.ShapeDtypeStruct((8, span_total), F32),
        in_specs=[vmem] * 8 + [hbm] * 2,
        out_specs=vmem,
        scratch_shapes=[
            pltpu.VMEM((n_ctx, kv_local, rows, HD), BF16),
            pltpu.VMEM((n_ctx, kv_local, HD, rows), BF16),
            pltpu.VMEM((n_ctx, kv_local, 8, rows), F32),
            pltpu.VMEM((n_ctx, kv_local, HD, rows), BF16),
            pltpu.VMEM((n_ctx, kv_local, 8, rows), F32),
            pltpu.VMEM((n_ctx, span_dev, heads_width), BF16),
            pltpu.VMEM(out_weight.shape, BF16),
            pltpu.VMEM((n_tp, tok_tp, cols), BF16),
            pltpu.VMEM((n_tp, tok_tp, cols), BF16),
            pltpu.VMEM((n_ctx, n_tp, 2, tok_tp // 2, cols), BF16),
            pltpu.VMEM((n_dev, 8, span_total), F32),
            pltpu.VMEM((span_total, 128), F32),
            pltpu.VMEM((slots, vocab_dev, chunk), BF16),
            pltpu.VMEM((vocab_dev, span_total), F32),
            pltpu.VMEM((n_dev, 8, span_total), F32),
            dma((n_ctx,)),
            dma((n_ctx,)),
            dma((n_ctx,)),
            dma((n_ctx,)),
            dma((n_ctx,)),
            dma((n_ctx,)),
            dma((n_ctx,)),
            dma((n_ctx,)),
            dma((n_tp,)),
            dma((n_tp,)),
            dma((y_sends,)),
            dma((n_dev * 2,)),
            dma((n_dev,)),
            dma((n_dev,)),
            dma((n_dev,)),
            dma((n_dev,)),
            dma,
            dma((slots,)),
        ],
        compiler_params=pltpu.CompilerParams(
            collective_id=0, has_side_effects=True, vmem_limit_bytes=60 * 1024 * 1024
        ),
        name="score_span",
    )(
        queries,
        cache_keys,
        cache_values.T,
        fresh_keys,
        fresh_values,
        residual,
        norm_gain[None, :],
        targets[None, :],
        out_weight,
        head_weight.T,
    )
    token_logprob = table[0]
    window_ends = jnp.cumsum(window_lengths)
    window_starts = window_ends - window_lengths
    positions = jnp.arange(span_total, dtype=jnp.int32)
    member = (positions[None, :] >= window_starts[:, None]) & (
        positions[None, :] < window_ends[:, None]
    )
    window_sums = jnp.sum(jnp.where(member, token_logprob[None, :], 0.0), axis=1)
    window_means = window_sums / window_lengths.astype(F32)
    first_token = lax.axis_index("ctx") * span_dev
    own_logprob = lax.dynamic_slice_in_dim(token_logprob, first_token, span_dev, 0)
    return (own_logprob, window_means)


def solution(mesh):
    in_specs = (
        P("ctx", "tp"),
        P("ctx", "tp"),
        P("ctx", "tp"),
        P("ctx", "tp"),
        P("ctx", "tp"),
        P("tp", "ctx"),
        P("tp", "ctx"),
        P("ctx"),
        P(None, ("ctx", "tp")),
        P(),
        P(),
    )
    out_specs = (P("ctx"), P())
    body = functools.partial(local, mesh.shape["ctx"], mesh.shape["tp"])
    return jax.shard_map(body, mesh=mesh, in_specs=in_specs, out_specs=out_specs, check_vma=False)
```

```python
import functools

import jax
import jax.numpy as jnp
from jax import lax
from jax.experimental import pallas as pl
from jax.experimental.pallas import tpu as pltpu
from jax.sharding import PartitionSpec as P

HD = 128
GROUP = 8
ONES = 16
LOG2E = 1.4426950408889634
EPSILON = 1e-05
NEGATIVE = -1e30
MESH = pl.DeviceIdType.MESH
F32 = jnp.float32
BF16 = jnp.bfloat16


def dot_nt(left, right):
    return lax.dot_general(
        left, right, (((1,), (1,)), ((), ())), preferred_element_type=F32
    )


def remote(src, dst, send_sem, recv_sem, device):
    return pltpu.make_async_remote_copy(
        src_ref=src,
        dst_ref=dst,
        send_sem=send_sem,
        recv_sem=recv_sem,
        device_id=device,
        device_id_type=MESH,
    )


def kernel(
    n_ctx,
    n_tp,
    slots,
    query_ref,
    key_ref,
    value_ref,
    fresh_key_ref,
    fresh_value_ref,
    residual_ref,
    gain_ref,
    target_ref,
    out_weight_ref,
    head_ref,
    result_ref,
    v_buf,
    fk_buf,
    fv_buf,
    q_buf,
    o_send,
    s_send,
    o_buf,
    s_buf,
    a_buf,
    w_buf,
    p_send,
    p_buf,
    y_buf,
    sq_buf,
    column_buf,
    h_buf,
    acc,
    st_buf,
    q_ss,
    q_rs,
    o_ss,
    o_rs,
    s_ss,
    s_rs,
    a_ss,
    a_rs,
    p_ss,
    p_rs,
    y_ss,
    y_rs,
    sq_ss,
    sq_rs,
    st_ss,
    st_rs,
    w_sem,
    h_sem,
):
    c = lax.axis_index("ctx")
    t = lax.axis_index("tp")
    n_dev = n_ctx * n_tp
    me = c * n_tp + t
    n_o = n_ctx // 2
    n_y = n_tp // 2
    o, i = c // 2, lax.rem(c, 2)
    y, k = t // 2, lax.rem(t, 2)
    across = (o * 2 + (1 - i), t)
    sides = [lax.rem(y + dy, n_y) * 2 + k for dy in range(1, n_y)]
    twin = (c, y * 2 + (1 - k))
    kv_local = key_ref.shape[1] // HD
    span_dev = query_ref.shape[0]
    rows = span_dev * GROUP
    keys = key_ref.shape[0]
    tok_tp = residual_ref.shape[0]
    cols = residual_ref.shape[1]
    vocab_dev, width = head_ref.shape
    n_tokens = n_ctx * span_dev
    half = tok_tp // 2
    scaling = HD ** (-0.5)

    def peer(step):
        return lax.rem(o + lax.rem(step, n_o), n_o) * 2 + lax.rem(i + step // n_o, 2)

    def fetch(j, slot):
        return pltpu.make_async_copy(
            head_ref.at[:, pl.ds(pl.multiple_of(peer(j) * cols, cols), cols)],
            h_buf.at[slot],
            h_sem.at[slot],
        )

    w_copy = pltpu.make_async_copy(out_weight_ref, w_buf, w_sem)
    w_copy.start()
    for j in range(slots):
        fetch(j, j).start()

    def other(step):
        index = lax.rem(me + step, n_dev)
        return (index // n_tp, lax.rem(index, n_tp))

    barrier = pltpu.get_barrier_semaphore()

    @pl.loop(1, n_dev)
    def _(step):
        pl.semaphore_signal(barrier, inc=1, device_id=other(step), device_id_type=MESH)

    pl.semaphore_wait(barrier, n_dev - 1)

    def row_copy(buf, send_sem, recv_sem, rank, sem, device):
        return remote(buf.at[rank], buf.at[rank], send_sem.at[sem], recv_sem.at[rank], device)

    def query_copy(rank, sem, device):
        return row_copy(q_buf, q_ss, q_rs, rank, sem, device)

    def partial_copies(rank, dst):
        return (
            remote(o_send.at[dst], o_buf.at[rank], o_ss.at[dst], o_rs.at[rank], (dst, t)),
            remote(s_send.at[dst], s_buf.at[rank], s_ss.at[dst], s_rs.at[rank], (dst, t)),
        )

    for kv in range(kv_local):
        for g in range(GROUP):
            lo = (kv * GROUP + g) * HD
            q_buf[c, kv, g * span_dev : (g + 1) * span_dev, :] = query_ref[:, lo : lo + HD]

    query_copy(c, n_o, across).start()

    @pl.loop(1, n_o)
    def _(step):
        query_copy(c, step, (peer(step), t)).start()

    key_block = min(1024, keys)
    for at in range(0, keys, key_block):
        for kv in range(kv_local):
            lo = kv * HD
            v_buf[kv, 0:HD, at : at + key_block] = value_ref[
                at : at + key_block, lo : lo + HD
            ].T
    fresh_rows = fk_buf.shape[0]
    fk_buf[...] = jnp.zeros(fk_buf.shape, BF16)
    fk_buf[0:span_dev, :] = fresh_key_ref[...]
    fv_buf[...] = jnp.zeros(fv_buf.shape, BF16)
    fv_buf[0:span_dev, :] = fresh_value_ref[...]
    for kv in range(kv_local):
        lo = kv * HD
        v_buf[kv, 0:HD, keys : keys + fresh_rows] = fv_buf[:, lo : lo + HD].T
        v_buf[kv, HD : HD + ONES, :] = jnp.ones((ONES, keys + fresh_rows), BF16)

    @pl.loop(0, n_ctx)
    def _(step):
        p = peer(step)

        @pl.when(step > 0)
        def _():
            query_copy(p, 0, across).wait_recv()

        @pl.when((step > 0) & (step < n_o))
        def _():
            query_copy(p, n_o + step, across).start()

        blocks = [(at, at + key_block) for at in range(0, keys, key_block)]
        blocks.append((keys, keys + fresh_rows))
        order = [(kv, at, to) for kv in range(kv_local) for at, to in blocks]

        def score(entry):
            kv, at, to = entry
            lo = kv * HD
            if at < keys:
                return dot_nt(key_ref[at:to, lo : lo + HD], q_buf[p, kv])
            s = dot_nt(fk_buf[:, lo : lo + HD], q_buf[p, kv])
            j = lax.broadcasted_iota(jnp.int32, s.shape, 0)
            token = lax.rem(lax.broadcasted_iota(jnp.int32, s.shape, 1), span_dev)
            seen = (p * span_dev + token >= c * span_dev + j) & (j < span_dev)
            return jnp.where(seen, s, NEGATIVE)

        coming = score(order[0])
        for index, (kv, at, to) in enumerate(order):
            s = coming
            if index + 1 < len(order):
                coming = score(order[index + 1])
            v = v_buf[kv, :, at:to]
            top = jnp.max(s, axis=0, keepdims=True)
            new_max = top if at == 0 else jnp.maximum(row_max, top)
            w = jnp.exp2(((s - new_max) * (scaling * LOG2E)).astype(BF16))
            part = jnp.dot(v, w, preferred_element_type=F32)
            if at == 0:
                weighted = part
            else:
                weighted = weighted * jnp.exp2((row_max - new_max) * (scaling * LOG2E)) + part
            row_max = new_max
            if to <= keys:
                continue
            row_sum = weighted[HD : HD + 1]
            weighted = weighted[0:HD]
            o_send[p, kv] = (weighted / row_sum).astype(BF16)
            s_send[p, kv, 0:4, :] = jnp.broadcast_to(row_max * scaling, (4, rows))
            s_send[p, kv, 4:8, :] = jnp.broadcast_to(row_sum, (4, rows))

        @pl.when(step > 0)
        def _():
            for copy in partial_copies(c, p):
                copy.start()

    o_buf[c] = o_send[c]
    s_buf[c] = s_send[c]

    @pl.loop(1, n_ctx)
    def _(step):
        p = peer(step)
        query_copy(c, step, across).wait_send()
        for copy in partial_copies(p, p):
            copy.wait_send()
            copy.wait_recv()

    for kv in range(kv_local):
        tops = [s_buf[src, kv, 0:1, :] for src in range(n_ctx)]
        best = functools.reduce(jnp.maximum, tops)
        total = jnp.zeros((1, rows), F32)
        mixed = jnp.zeros((HD, rows), F32)
        for src in range(n_ctx):
            share = s_buf[src, kv, 4:5, :] * jnp.exp(tops[src] - best)
            total = total + share
            mixed = mixed + o_buf[src, kv].astype(F32) * share
        attended = (mixed / total).T.astype(BF16)
        for g in range(GROUP):
            lo = (kv * GROUP + g) * HD
            a_buf[c, :, lo : lo + HD] = attended[g * span_dev : (g + 1) * span_dev]

    def attended_copy(rank, sem, device):
        return row_copy(a_buf, a_ss, a_rs, rank, sem, device)

    attended_copy(c, n_o, across).start()

    @pl.loop(1, n_o)
    def _(step):
        attended_copy(c, step, (peer(step), t)).start()

    acc[...] = jnp.zeros(acc.shape, F32)
    w_copy.wait()

    @pl.loop(1, n_o)
    def _(step):
        attended_copy(peer(step), 0, across).wait_recv()
        attended_copy(peer(step), n_o + step, across).start()

    @pl.loop(n_o, n_ctx)
    def _(step):
        attended_copy(peer(step), 0, across).wait_recv()

    tile = min(256, cols)
    for at in range(0, cols, tile):
        product = jnp.dot(
            a_buf[...].reshape(n_tokens, a_buf.shape[2]),
            w_buf[:, at : at + tile],
            preferred_element_type=F32,
        ).astype(BF16)
        p_send[:, :, at : at + tile] = product.reshape(n_tp, tok_tp, tile)

    def product_copy(rank, dst):
        return remote(p_send.at[dst], p_buf.at[rank], p_ss.at[dst], p_rs.at[rank], (c, dst))

    for step in range(1, n_tp):
        product_copy(t, lax.rem(t + step, n_tp)).start()
    p_buf[t] = p_send[t]
    for step in range(1, n_tp):
        dst = lax.rem(t + step, n_tp)
        product_copy(dst, dst).wait_recv()

    stream = residual_ref[...].astype(F32)
    for src in range(n_tp):
        stream = stream + p_buf[src].astype(F32)
    gained = (stream * gain_ref[...].astype(F32)).astype(BF16)
    y_buf[c, t, 0] = gained[:half]
    y_buf[c, t, 1] = gained[half:]
    squares = jnp.sum(stream * stream, axis=1, keepdims=True)
    column_buf[...] = jnp.zeros(column_buf.shape, F32)
    column_buf[pl.ds(pl.multiple_of(t * tok_tp, tok_tp), tok_tp), :] = jnp.broadcast_to(
        squares, (tok_tp, 128)
    )
    sq_buf[me] = column_buf[...].T[0:8]

    def block_copy(cc, tt, h, device, sem):
        return remote(
            y_buf.at[cc, tt, h],
            y_buf.at[cc, tt, h],
            y_ss.at[sem],
            y_rs.at[(cc * n_tp + tt) * 2 + h],
            device,
        )

    def arrive(cc, tt, h):
        block_copy(cc, tt, h, across, 0).wait_recv()

    n_s = n_y - 1
    forwards = 4 + 2 * n_s
    relays = 2 + 4 * n_s
    base_relay = 2 * (n_o - 1) + n_o * forwards
    base_last = base_relay + n_o * relays
    y_sends = base_last + n_o * 2 * n_s

    def forward(dz):
        cc = peer(dz)
        sem = 2 * (n_o - 1) + dz * forwards
        block_copy(cc, t, 0, across, sem).start()
        for at, side in enumerate(sides):
            block_copy(cc, t, 1, (c, side), sem + 4 + 2 * at).start()
        for h in range(2):
            block_copy(cc, t, h, twin, sem + 1 + h).start()
        for at, side in enumerate(sides):
            block_copy(cc, t, 0, (c, side), sem + 5 + 2 * at).start()
        block_copy(cc, t, 1, across, sem + 3).start()

    def relay(dz):
        near, far = peer(dz), peer(n_o + dz)
        sem = base_relay + dz * relays
        arrive(far, t, 0)
        for at, side in enumerate(sides):
            block_copy(far, t, 0, (c, side), sem + 2 + 4 * at).start()
        block_copy(far, t, 0, twin, sem).start()
        for at, side in enumerate(sides):
            arrive(near, side, 1)
            block_copy(near, side, 1, across, sem + 3 + 4 * at).start()
            block_copy(near, side, 1, twin, sem + 4 + 4 * at).start()
            arrive(near, side, 0)
            block_copy(near, side, 0, twin, sem + 5 + 4 * at).start()
        arrive(far, t, 1)
        block_copy(far, t, 1, twin, sem + 1).start()

    def last_relay(dz):
        far = peer(n_o + dz)
        sem = base_last + dz * 2 * n_s
        for at, side in enumerate(sides):
            for h in range(2):
                arrive(far, side, h)
                block_copy(far, side, h, twin, sem + 2 * at + h).start()

    def from_twin(cc):
        for yy in range(n_y):
            for h in range(2):
                arrive(cc, yy * 2 + (1 - k), h)

    def multiply(j):
        slot = lax.rem(j, slots)
        fetch(j, slot).wait()
        left = y_buf[peer(j)].reshape(n_tokens, cols)
        for at in range(0, vocab_dev, 512):
            to = min(at + 512, vocab_dev)
            acc[at:to, :] += dot_nt(h_buf[slot, at:to, :], left)

        @pl.when(j + slots < n_ctx)
        def _():
            fetch(j + slots, slot).start()

    for dz in range(1, n_o):
        for h in range(2):
            block_copy(c, t, h, (peer(dz), t), 2 * (dz - 1) + h).start()
    forward(0)

    def square_copy(rank, step, device):
        return remote(sq_buf.at[rank], sq_buf.at[rank], sq_ss.at[step], sq_rs.at[rank], device)

    @pl.loop(1, n_dev)
    def _(step):
        square_copy(me, step, other(step)).start()

    @pl.loop(1, n_o)
    def _(dz):
        for h in range(2):
            arrive(peer(dz), t, h)
        forward(dz)

    relay(0)

    @pl.loop(0, n_o)
    def _(dz):
        @pl.when(dz + 1 < n_o)
        def _():
            relay(dz + 1)

        from_twin(peer(dz))
        multiply(dz)

    last_relay(0)

    @pl.loop(0, n_o)
    def _(dz):
        @pl.when(dz + 1 < n_o)
        def _():
            last_relay(dz + 1)

        from_twin(peer(n_o + dz))
        multiply(n_o + dz)

    @pl.loop(1, n_dev)
    def _(step):
        square_copy(lax.rem(me + step, n_dev), step, other(step)).wait_recv()

    vocab_start = me * vocab_dev
    total = sq_buf[0, 0:1]
    for rank in range(1, n_dev):
        total = total + sq_buf[rank, 0:1]
    scale = lax.rsqrt(total / width + EPSILON)
    top = jnp.max(acc[...] * scale, axis=0, keepdims=True)
    mass = jnp.zeros((1, n_tokens), F32)
    mark = jnp.zeros((1, n_tokens), F32)
    for at in range(0, vocab_dev, 512):
        to = min(at + 512, vocab_dev)
        logits = acc[at:to, :] * scale
        mass = mass + jnp.sum(jnp.exp(logits - top), axis=0, keepdims=True)
        entry = vocab_start + at + lax.broadcasted_iota(jnp.int32, logits.shape, 0)
        hit = target_ref[...] == entry
        mark = mark + jnp.sum(jnp.where(hit, logits, 0.0), axis=0, keepdims=True)
    st_buf[me, 0:2, :] = jnp.broadcast_to(top, (2, n_tokens))
    st_buf[me, 2:4, :] = jnp.broadcast_to(mass, (2, n_tokens))
    st_buf[me, 4:8, :] = jnp.broadcast_to(mark, (4, n_tokens))

    def stat_copy(rank, step, device):
        return remote(st_buf.at[rank], st_buf.at[rank], st_ss.at[step], st_rs.at[rank], device)

    @pl.loop(1, n_dev)
    def _(step):
        stat_copy(me, step, other(step)).start()

    @pl.loop(0, y_sends)
    def _(sem):
        block_copy(c, t, 0, across, sem).wait_send()

    @pl.loop(1, n_ctx)
    def _(step):
        attended_copy(c, step, across).wait_send()

    for step in range(1, n_tp):
        product_copy(t, lax.rem(t + step, n_tp)).wait_send()

    @pl.loop(1, n_dev)
    def _(step):
        square_copy(me, step, other(step)).wait_send()
        stat_copy(me, step, other(step)).wait_send()
        stat_copy(lax.rem(me + step, n_dev), step, other(step)).wait_recv()

    tops = [st_buf[rank, 0:1, :] for rank in range(n_dev)]
    top = functools.reduce(jnp.maximum, tops)
    mass = jnp.zeros((1, n_tokens), F32)
    mark = jnp.zeros((1, n_tokens), F32)
    for rank in range(n_dev):
        mass = mass + st_buf[rank, 2:3, :] * jnp.exp(tops[rank] - top)
        mark = mark + st_buf[rank, 4:5, :]
    result_ref[...] = jnp.broadcast_to(mark - (top + jnp.log(mass)), result_ref.shape)


def local(
    n_ctx,
    n_tp,
    queries,
    cache_keys,
    cache_values,
    span_keys,
    span_values,
    out_weight,
    residual,
    norm_gain,
    head_weight,
    targets,
    window_lengths,
):
    span_dev = queries.shape[0]
    kv_local = cache_keys.shape[1] // HD
    rows = GROUP * span_dev
    span_total = span_dev * n_ctx
    n_dev = n_ctx * n_tp
    heads_width = queries.shape[1]
    tok_tp, cols = residual.shape
    vocab_dev = head_weight.shape[1]
    slots = min(3, n_ctx)
    fresh = -(-span_dev // 128) * 128
    vmem = pl.BlockSpec(memory_space=pltpu.VMEM)
    hbm = pl.BlockSpec(memory_space=pl.ANY)
    dma = pltpu.SemaphoreType.DMA
    n_o, n_y = n_ctx // 2, n_tp // 2
    y_sends = 2 * (n_o - 1) + n_o * (4 + 2 * (n_y - 1)) + n_o * (2 + 4 * (n_y - 1)) + n_ctx * (n_y - 1)
    table = pl.pallas_call(
        functools.partial(kernel, n_ctx, n_tp, slots),
        out_shape=jax.ShapeDtypeStruct((8, span_total), F32),
        in_specs=[vmem] * 8 + [hbm] * 2,
        out_specs=vmem,
        scratch_shapes=[
            pltpu.VMEM((kv_local, HD + ONES, cache_values.shape[0] + fresh), BF16),
            pltpu.VMEM((fresh, span_keys.shape[1]), BF16),
            pltpu.VMEM((fresh, span_keys.shape[1]), BF16),
            pltpu.VMEM((n_ctx, kv_local, rows, HD), BF16),
            pltpu.VMEM((n_ctx, kv_local, HD, rows), BF16),
            pltpu.VMEM((n_ctx, kv_local, 8, rows), F32),
            pltpu.VMEM((n_ctx, kv_local, HD, rows), BF16),
            pltpu.VMEM((n_ctx, kv_local, 8, rows), F32),
            pltpu.VMEM((n_ctx, span_dev, heads_width), BF16),
            pltpu.VMEM(out_weight.shape, BF16),
            pltpu.VMEM((n_tp, tok_tp, cols), BF16),
            pltpu.VMEM((n_tp, tok_tp, cols), BF16),
            pltpu.VMEM((n_ctx, n_tp, 2, tok_tp // 2, cols), BF16),
            pltpu.VMEM((n_dev, 8, span_total), F32),
            pltpu.VMEM((span_total, 128), F32),
            pltpu.VMEM((slots, vocab_dev, cols), BF16),
            pltpu.VMEM((vocab_dev, span_total), F32),
            pltpu.VMEM((n_dev, 8, span_total), F32),
            dma((n_ctx,)),
            dma((n_ctx,)),
            dma((n_ctx,)),
            dma((n_ctx,)),
            dma((n_ctx,)),
            dma((n_ctx,)),
            dma((n_ctx,)),
            dma((n_ctx,)),
            dma((n_tp,)),
            dma((n_tp,)),
            dma((y_sends,)),
            dma((n_dev * 2,)),
            dma((n_dev,)),
            dma((n_dev,)),
            dma((n_dev,)),
            dma((n_dev,)),
            dma,
            dma((slots,)),
        ],
        compiler_params=pltpu.CompilerParams(
            collective_id=0, has_side_effects=True, vmem_limit_bytes=60 * 1024 * 1024
        ),
        name="score_span",
    )(
        queries,
        cache_keys,
        cache_values,
        span_keys,
        span_values,
        residual,
        norm_gain[None, :],
        targets[None, :],
        out_weight,
        head_weight.T,
    )
    token_logprob = table[0]
    window_ends = jnp.cumsum(window_lengths)
    window_starts = window_ends - window_lengths
    positions = jnp.arange(span_total, dtype=jnp.int32)
    member = (positions[None, :] >= window_starts[:, None]) & (
        positions[None, :] < window_ends[:, None]
    )
    window_sums = jnp.sum(jnp.where(member, token_logprob[None, :], 0.0), axis=1)
    window_means = window_sums / window_lengths.astype(F32)
    first_token = lax.axis_index("ctx") * span_dev
    own_logprob = lax.dynamic_slice_in_dim(token_logprob, first_token, span_dev, 0)
    return (own_logprob, window_means)


def solution(mesh):
    in_specs = (
        P("ctx", "tp"),
        P("ctx", "tp"),
        P("ctx", "tp"),
        P("ctx", "tp"),
        P("ctx", "tp"),
        P("tp", "ctx"),
        P("tp", "ctx"),
        P("ctx"),
        P(None, ("ctx", "tp")),
        P(),
        P(),
    )
    out_specs = (P("ctx"), P())
    body = functools.partial(local, mesh.shape["ctx"], mesh.shape["tp"])
    return jax.shard_map(body, mesh=mesh, in_specs=in_specs, out_specs=out_specs, check_vma=False)
```
